32 devices in a mesh: outer: 2 (over x), member: 16 (over z, y, core).
Axes of the slice: x: 2, y: 2, z: 4, core: 2. Of those that a mesh axis runs over, the one named last changes fastest.
Arguments:
- vectors: bfloat16 [4096, 1024], P(('outer', 'member')), may hold values from -64 to 64
- list_ids: int32 [4096], P(('outer', 'member')), may hold values from 0 to 32767, as said below
- coarse_centroids: bfloat16 [32768, 1024], P('member'), may hold values from -3 to 3
- codebook: bfloat16 [16, 64, 2048], P('outer'), may hold values from -2 to 6
Outputs:
- reconstructed: bfloat16 [4096, 1024], P(('outer', 'member'))
- codebook_grad: float32 [16, 64, 2048], P('outer')
The draws below stay inside these ranges and needn't reach their ends.
Inputs may be any that keep to these rules, and one draw needn't show every extreme that they name: `list_ids`: member j owns lists j * 2048 to (j + 1) * 2048 - 1. The 128 vectors of one device (an aligned block of the array) name lists of at most 16 vectors owned by any one member; in every pod one member owns the lists of exactly 16 vectors of every device of that pod.
All inputs are finite; a program needn't handle non-finite values.
Results may differ from the reference program's by a relative error of at most 0.0077.
Values may be sent and summed in bfloat16 or wider, within the bound.
A program may use at most 128 MiB of HBM per device.

```python
import jax
import jax.numpy as jnp
from jax import lax

D = 1024
M = 16
SUB = 64
K = 2048
NLIST = 32768
V_DEV = 128
LIST_DEV = 2048
CAP = 16
VECTORS = 4096
N_OUTER = 2
N_MEMBER = 16


def list_draw(key):
    base_key = jax.random.fold_in(key, 5)
    sub_keys = jax.random.split(base_key, 5)
    hot_pod = jax.random.randint(sub_keys[0], (N_OUTER,), 0, N_MEMBER)
    hot_block = jnp.repeat(hot_pod, N_MEMBER)
    spare = (N_MEMBER - 1) * CAP

    def one_device(block_key, hot_member):
        first_key, second_key = jax.random.split(block_key)
        chosen = jax.random.permutation(first_key, spare)[:V_DEV - CAP]
        member_of = (chosen // CAP).astype(jnp.int32)
        member_of = member_of + (member_of >= hot_member).astype(jnp.int32)
        owners = jnp.concatenate([jnp.full((CAP,), hot_member, jnp.int32), member_of])
        return jax.random.permutation(second_key, owners)
    owners = jax.vmap(one_device)(jax.random.split(sub_keys[1], N_OUTER * N_MEMBER), hot_block).reshape(-1)
    first = jax.random.randint(sub_keys[2], (VECTORS,), 0, LIST_DEV)
    second = jax.random.randint(sub_keys[3], (VECTORS,), 0, LIST_DEV)
    offsets = jax.random.randint(sub_keys[4], (N_MEMBER,), 0, LIST_DEV)
    local_list = (first * second // LIST_DEV + offsets[owners]) % LIST_DEV
    return (owners * LIST_DEV + local_list).astype(jnp.int32)


def coarse_table(key):
    table_key = jax.random.fold_in(key, 11)
    return 0.5 * jnp.clip(jax.random.normal(table_key, (NLIST, D), jnp.float32), -6.0, 6.0)


def plant_axes(key):
    plant_key = jax.random.fold_in(key, 17)
    second_key = jax.random.fold_in(plant_key, 1)
    lead_code = jax.random.randint(second_key, (M,), 0, K)
    return lead_code


def draw_list_ids(key, part):
    shared = list_draw(key)
    return shared


def draw_coarse_centroids(key, part):
    shared = coarse_table(key)
    return shared.astype(jnp.bfloat16)


def draw_codebook(key, part):
    lead_code = plant_axes(key)
    key = jax.random.fold_in(key, 23)
    mixing = 0.0
    drawn = 0.25 * jnp.clip(jax.random.normal(key, (M, SUB, K), jnp.float32), -6.0, 6.0)
    code_index = jnp.arange(K)[None, None, :]
    first_code = lead_code[:, None, None]
    second_code = (first_code + 1) % K
    chosen = ((code_index == first_code) | (code_index == second_code)).astype(jnp.float32) * mixing
    return (drawn * (1.0 - chosen)).astype(jnp.bfloat16)


def draw_vectors(key, part):
    list_rows = list_draw(key)
    table = coarse_table(key)
    key = jax.random.fold_in(key, 29)
    sub_keys = jax.random.split(key, 2)
    noise = jnp.clip(jax.random.normal(sub_keys[1], (VECTORS, D), jnp.float32), -6.0, 6.0)
    lifting = 0.0
    row_index = jnp.arange(VECTORS)
    picked = (row_index % 97 == 3).astype(jnp.float32) * lifting
    offset_rows = noise * (1.0 - picked[:, None])
    return (table[list_rows] + offset_rows).astype(jnp.bfloat16)


def setup_inputs(seed: int = 0) -> dict:
    splits = jax.random.split(jax.random.key(seed), 5)
    return {
        "vectors": draw_vectors(jax.random.fold_in(splits[4], 71), 0),
        "list_ids": draw_list_ids(jax.random.fold_in(splits[4], 71), 0),
        "coarse_centroids": draw_coarse_centroids(jax.random.fold_in(splits[4], 71), 0),
        "codebook": draw_codebook(jax.random.fold_in(splits[4], 71), 0),
    }


logit_scale = 0.5


def reference(vectors, list_ids, coarse_centroids, codebook):
    centroid_rows = jnp.take(coarse_centroids, list_ids, axis=0)
    residual = (vectors.astype(jnp.float32) - centroid_rows.astype(jnp.float32)).astype(jnp.bfloat16)
    residual = lax.optimization_barrier(residual).astype(jnp.float32)
    codes = codebook.astype(jnp.float32)
    code_norm = jnp.sum(codes * codes, axis=1)
    block_rows = 1024 if VECTORS % 1024 == 0 else VECTORS

    def one_block(running, row_piece):
        split_rows = row_piece.reshape(block_rows, M, SUB)
        logits = logit_scale * (2.0 * jnp.einsum('bsd,sdk->bsk', split_rows, codes) - code_norm[None])
        weights = jax.nn.softmax(logits, axis=-1).astype(jnp.bfloat16)
        weights = lax.optimization_barrier(weights).astype(jnp.float32)
        rebuilt = jnp.einsum('bsk,sdk->bsd', weights, codes).astype(jnp.bfloat16)
        code_sums = running[0] + jnp.einsum('bsd,bsk->sdk', split_rows, weights)
        counts = running[1] + jnp.sum(weights, axis=0)
        return (code_sums, counts), rebuilt.reshape(block_rows, D)

    start = (jnp.zeros((M, SUB, K), jnp.float32), jnp.zeros((M, K), jnp.float32))
    (code_sums, counts), rebuilt = lax.scan(one_block, start, residual.reshape(-1, block_rows, D))
    rebuilt = lax.optimization_barrier(rebuilt.reshape(VECTORS, D)).astype(jnp.float32)
    reconstructed = (centroid_rows.astype(jnp.float32) + rebuilt).astype(jnp.bfloat16)
    codebook_grad = (2.0 * K / VECTORS) * (counts[:, None, :] * codes - code_sums)
    return reconstructed, codebook_grad
```

```python
import functools
import math

import jax
import jax.numpy as jnp
from jax import lax
from jax.experimental import pallas as pl
from jax.experimental.pallas import tpu as pltpu
from jax.sharding import PartitionSpec as P

LOG2E = math.log2(math.e)
F32, BF16 = jnp.float32, jnp.bfloat16


def pieces(x):
    hi = x.astype(BF16)
    rest = x - hi.astype(F32)
    mid = rest.astype(BF16)
    low = (rest - mid.astype(F32)).astype(BF16)
    return hi, mid, low


def one_subspace(code, res_t, scale):
    rows = res_t.shape[1]
    codes = code.shape[1]
    code_wide = code.astype(F32)
    norm = (-0.5 * LOG2E) * jnp.sum(code_wide * code_wide, axis=0, keepdims=True)
    hi, mid, low = pieces(norm)
    row_index = lax.broadcasted_iota(jnp.int32, (16, codes), 0)
    tail = jnp.where(
        row_index == 0,
        hi.astype(F32),
        jnp.where(row_index == 1, mid.astype(F32), jnp.where(row_index == 2, low.astype(F32), 0.0)),
    ).astype(BF16)
    right = jnp.concatenate([code, code, code, tail], axis=0)
    ones = jnp.ones((16, rows), BF16)
    left = jnp.concatenate([*pieces(res_t.astype(F32) * LOG2E), ones], axis=0)
    logits = lax.dot_general(left, right, (((0,), (0,)), ((), ())), preferred_element_type=F32)
    top = jnp.max(logits, axis=1, keepdims=True)
    raised = jnp.exp2(logits - top)
    total = jnp.sum(raised, axis=1, keepdims=True)
    weights = (raised * (1.0 / total)).astype(BF16)
    rebuilt_t = lax.dot_general(code, weights, (((1,), (1,)), ((), ())), preferred_element_type=F32)
    sums = jnp.dot(jnp.concatenate([res_t, ones], axis=0), weights, preferred_element_type=F32)
    sub = code.shape[0]
    counts = sums[sub : sub + 1, :]
    return rebuilt_t, scale * (counts * code_wide - sums[:sub, :])


def quantize_kernel(scale, sub, res_ref, cent_ref, code_ref, out_ref, grad_ref, res_t, reb_t):
    spaces = code_ref.shape[0]
    res_t[...] = res_ref[...].astype(F32).T.astype(BF16)

    @pl.loop(0, spaces)
    def _(space):
        at = pl.ds(pl.multiple_of(space * sub, sub), sub)
        rebuilt_t, grad = one_subspace(code_ref[space], res_t[at, :], scale)
        reb_t[at, :] = rebuilt_t
        grad_ref[space] = grad.astype(BF16)

    rebuilt = reb_t[...].T.astype(BF16).astype(F32)
    out_ref[...] = (cent_ref[...].astype(F32) + rebuilt).astype(BF16)


def quantize(scale, residual, cent, codebook):
    rows, cols = residual.shape
    spaces, sub, codes = codebook.shape
    vmem = pl.BlockSpec(memory_space=pltpu.VMEM)
    return pl.pallas_call(
        functools.partial(quantize_kernel, scale, sub),
        out_shape=(
            jax.ShapeDtypeStruct((rows, cols), BF16),
            jax.ShapeDtypeStruct((spaces, sub, codes), BF16),
        ),
        in_specs=[vmem] * 3,
        out_specs=(vmem, vmem),
        scratch_shapes=[pltpu.VMEM((cols, rows), BF16), pltpu.VMEM((cols, rows), F32)],
        compiler_params=pltpu.CompilerParams(vmem_limit_bytes=48 * 2**20),
    )(residual, cent, codebook)


def on_device(vectors, list_ids, coarse_centroids, codebook):
    rows_dev, row_width = vectors.shape
    members = lax.axis_size("member")
    outers = lax.axis_size("outer")
    lists_dev = coarse_centroids.shape[0]
    capacity = 2 * rows_dev // members
    cols = row_width // outers
    me = lax.axis_index("member")
    outer = lax.axis_index("outer")
    pair_rows = lax.all_to_all(vectors, "outer", split_axis=1, concat_axis=0, tiled=True)
    ids_all = lax.all_gather(list_ids, ("member", "outer"), axis=0, tiled=False)
    ids_all = ids_all.reshape(members * outers, rows_dev)
    ids_pair = lax.dynamic_slice_in_dim(ids_all, me * outers, outers, 0)
    before = jnp.triu(jnp.ones((rows_dev, rows_dev), BF16), 1)

    local = ids_all - me * lists_dev
    own = (local >= 0) & (local < lists_dev)
    rank = jnp.dot(own.astype(BF16), before, preferred_element_type=F32).astype(jnp.int32)
    slot = jnp.arange(capacity, dtype=jnp.int32)
    picked = own[:, None, :] & (rank[:, None, :] == slot[None, :, None])
    index = jnp.sum(jnp.where(picked, local[:, None, :], 0), axis=2).reshape(-1)
    onehot = (index[:, None] == jnp.arange(lists_dev, dtype=jnp.int32)[None, :]).astype(BF16)
    table = lax.dynamic_slice_in_dim(coarse_centroids, outer * cols, cols, 1)
    sent = jnp.dot(onehot, table, preferred_element_type=BF16)
    sent = sent.reshape(members, outers * capacity, cols)
    got = lax.all_to_all(sent, "member", split_axis=0, concat_axis=0, tiled=True)
    got = got.reshape(members, outers, capacity, cols)

    owner = ids_pair // lists_dev
    owned = owner[:, :, None] == jnp.arange(members, dtype=jnp.int32)
    count = jnp.einsum("nm,onj->omj", before, owned.astype(BF16), preferred_element_type=F32)
    rank = count.astype(jnp.int32)
    place = owned[:, :, :, None] & (rank[:, :, :, None] == slot)
    cent = jnp.einsum("onjr,jord->ond", place.astype(BF16), got, preferred_element_type=BF16)
    cent = cent.reshape(outers * rows_dev, cols)
    residual = (pair_rows.astype(F32) - cent.astype(F32)).astype(BF16)

    scale = 2.0 * codebook.shape[2] / (rows_dev * members * outers)
    full, partial = quantize(scale, residual, cent, codebook)
    result = lax.all_to_all(full, "outer", split_axis=0, concat_axis=1, tiled=True)
    gradient = reduce_member(partial)
    return (result, gradient)


def reduce_member(partial):
    flat = partial.reshape(-1, partial.shape[2])
    mine = lax.psum_scatter(flat, "member", scatter_dimension=0, tiled=True)
    return lax.all_gather(mine, "member", axis=0, tiled=True).reshape(partial.shape).astype(F32)


def solution(mesh):
    return jax.shard_map(
        on_device,
        mesh=mesh,
        in_specs=(
            P(("outer", "member"), None),
            P(("outer", "member")),
            P("member", None),
            P("outer", None, None),
        ),
        out_specs=(P(("outer", "member"), None), P("outer", None, None)),
        check_vma=False,
    )
```

```python
import functools
import math

import jax
import jax.numpy as jnp
from jax import lax
from jax.experimental import pallas as pl
from jax.experimental.pallas import tpu as pltpu
from jax.sharding import PartitionSpec as P

MESH = pl.DeviceIdType.MESH
LOG2E = math.log2(math.e)
F32, BF16 = jnp.float32, jnp.bfloat16


def pieces(x):
    hi = x.astype(BF16)
    rest = x - hi.astype(F32)
    mid = rest.astype(BF16)
    low = (rest - mid.astype(F32)).astype(BF16)
    return hi, mid, low


def one_subspace(code, res_t, scale):
    rows = res_t.shape[1]
    codes = code.shape[1]
    code_wide = code.astype(F32)
    norm = (-0.5 * LOG2E) * jnp.sum(code_wide * code_wide, axis=0, keepdims=True)
    hi, mid, low = pieces(norm)
    row_index = lax.broadcasted_iota(jnp.int32, (16, codes), 0)
    tail = jnp.where(
        row_index == 0,
        hi.astype(F32),
        jnp.where(row_index == 1, mid.astype(F32), jnp.where(row_index == 2, low.astype(F32), 0.0)),
    ).astype(BF16)
    right = jnp.concatenate([code, code, code, tail], axis=0)
    ones = jnp.ones((16, rows), BF16)
    left = jnp.concatenate([*pieces(res_t.astype(F32) * LOG2E), ones], axis=0)
    logits = lax.dot_general(left, right, (((0,), (0,)), ((), ())), preferred_element_type=F32)
    top = jnp.max(logits, axis=1, keepdims=True)
    raised = jnp.exp2(logits - top)
    total = jnp.sum(raised, axis=1, keepdims=True)
    weights = (raised * (1.0 / total)).astype(BF16)
    rebuilt_t = lax.dot_general(code, weights, (((1,), (1,)), ((), ())), preferred_element_type=F32)
    sums = jnp.dot(jnp.concatenate([res_t, ones], axis=0), weights, preferred_element_type=F32)
    sub = code.shape[0]
    counts = sums[sub : sub + 1, :]
    return rebuilt_t, scale * (counts * code_wide - sums[:sub, :])


def later_on(axis, step):
    size = lax.axis_size(axis)
    return lax.rem(lax.axis_index(axis) + step, size)


def greet(axis_targets):
    barrier = pltpu.get_barrier_semaphore()
    for target in axis_targets:
        pl.semaphore_signal(barrier, inc=1, device_id=target, device_id_type=MESH)
    return barrier


def fetch_kernel(
    capacity,
    ids_ref,
    vec_ref,
    table_hbm,
    res_ref,
    cent_ref,
    table,
    ids_pair,
    ids_all,
    vec_got,
    sent,
    got,
    table_sem,
    pair_send,
    pair_recv,
    vec_send,
    vec_recv,
    ids_send,
    ids_recv,
    row_send,
    row_recv,
):
    members, outers = lax.axis_size("member"), lax.axis_size("outer")
    me, outer = lax.axis_index("member"), lax.axis_index("outer")
    lists_dev, cols = table.shape
    rows_dev = vec_ref.shape[0]
    block = outers * capacity
    slots = members * block

    def part(index):
        return pl.ds(pl.multiple_of(index * cols, cols), cols)

    def block_of(index):
        return pl.ds(pl.multiple_of(index * block, block), block)

    table_copy = pltpu.make_async_copy(table_hbm.at[:, part(outer)], table, table_sem)
    table_copy.start()
    barrier = greet([{"outer": later_on("outer", step)} for step in range(1, outers)])

    @pl.loop(1, members)
    def _(step):
        pl.semaphore_signal(
            barrier, inc=1, device_id={"member": later_on("member", step)}, device_id_type=MESH
        )

    ids_pair[outer] = ids_ref[...]
    vec_got[outer] = vec_ref[:, part(outer)]
    pl.semaphore_wait(barrier, outers + members - 2)

    def outer_copies(step):
        target = later_on("outer", step)
        ids_copy = pltpu.make_async_remote_copy(
            src_ref=ids_ref,
            dst_ref=ids_pair.at[outer],
            send_sem=pair_send.at[step],
            recv_sem=pair_recv.at[step],
            device_id={"outer": target},
            device_id_type=MESH,
        )
        vec_copy = pltpu.make_async_remote_copy(
            src_ref=vec_ref.at[:, part(target)],
            dst_ref=vec_got.at[outer],
            send_sem=vec_send.at[step],
            recv_sem=vec_recv.at[step],
            device_id={"outer": target},
            device_id_type=MESH,
        )
        return ids_copy, vec_copy

    outer_pairs = [outer_copies(step) for step in range(1, outers)]
    for ids_copy, _ in outer_pairs:
        ids_copy.start()
    for ids_copy, _ in outer_pairs:
        ids_copy.wait()

    def ids_copy_of(step):
        return pltpu.make_async_remote_copy(
            src_ref=ids_pair,
            dst_ref=ids_all.at[me],
            send_sem=ids_send.at[step],
            recv_sem=ids_recv.at[step],
            device_id={"member": later_on("member", step)},
            device_id_type=MESH,
        )

    @pl.loop(1, members)
    def _(step):
        ids_copy_of(step).start()

    for _, vec_copy in outer_pairs:
        vec_copy.start()

    ids_all[me] = ids_pair[...]
    row_index = lax.broadcasted_iota(jnp.int32, (rows_dev, rows_dev), 0)
    col_index = lax.broadcasted_iota(jnp.int32, (rows_dev, rows_dev), 1)
    before = jnp.where(row_index < col_index, 1.0, 0.0).astype(BF16)
    slot = lax.broadcasted_iota(jnp.int32, (slots, rows_dev), 0)
    slot_rank = lax.rem(slot, capacity).astype(F32)

    def picked(local):
        own = (local >= 0) & (local < lists_dev)
        rank = jnp.dot(jnp.where(own, 1.0, 0.0).astype(BF16), before, preferred_element_type=F32)
        return own & (rank == slot_rank)

    @pl.loop(1, members)
    def _(step):
        ids_copy_of(step).wait()

    ids = ids_all[...].reshape(members * outers, 1, rows_dev)
    ids = jnp.broadcast_to(ids, (members * outers, capacity, rows_dev)).reshape(slots, rows_dev)
    local = ids - me * lists_dev
    index = jnp.sum(jnp.where(picked(local), local.astype(F32), 0.0), axis=1, keepdims=True)
    lists = lax.broadcasted_iota(jnp.int32, (slots, lists_dev), 1)
    onehot = jnp.where(lists == index.astype(jnp.int32), 1.0, 0.0).astype(BF16)
    table_copy.wait()
    sent[...] = jnp.dot(onehot, table[...], preferred_element_type=F32).astype(BF16)

    def row_copy_of(step):
        target = later_on("member", step)
        return pltpu.make_async_remote_copy(
            src_ref=sent.at[block_of(target)],
            dst_ref=got.at[block_of(me)],
            send_sem=row_send.at[step],
            recv_sem=row_recv.at[step],
            device_id={"member": target},
            device_id_type=MESH,
        )

    @pl.loop(1, members)
    def _(step):
        row_copy_of(step).start()

    got[block_of(me)] = sent[block_of(me)]
    slot_owner = lax.div(slot, block)
    slot_outer = lax.rem(lax.div(slot, capacity), outers)
    places = []
    for source in range(outers):
        wanted = jnp.broadcast_to(ids_pair[source], (slots, rows_dev)) - slot_owner * lists_dev
        place = picked(wanted) & (slot_outer == source)
        places.append(jnp.where(place, 1.0, 0.0).T.astype(BF16))

    for _, vec_copy in outer_pairs:
        vec_copy.wait()

    @pl.loop(1, members)
    def _(step):
        row_copy_of(step).wait()

    for source in range(outers):
        cent = jnp.dot(places[source], got[...], preferred_element_type=F32)
        at = pl.ds(source * rows_dev, rows_dev)
        cent_ref[at, :] = cent.astype(BF16)
        res_ref[at, :] = (vec_got[source].astype(F32) - cent).astype(BF16)


def fetch(vectors, list_ids, coarse_centroids):
    rows_dev, row_width = vectors.shape
    members, outers = lax.axis_size("member"), lax.axis_size("outer")
    lists_dev = coarse_centroids.shape[0]
    capacity = max(2 * rows_dev // members, 16 // outers, 8)
    cols = row_width // outers
    slots = members * outers * capacity
    vmem = pl.BlockSpec(memory_space=pltpu.VMEM)
    dma = pltpu.SemaphoreType.DMA
    out = jax.ShapeDtypeStruct((outers * rows_dev, cols), BF16)
    return pl.pallas_call(
        functools.partial(fetch_kernel, capacity),
        out_shape=(out, out),
        in_specs=[vmem, vmem, pl.BlockSpec(memory_space=pl.ANY)],
        out_specs=(vmem, vmem),
        scratch_shapes=[
            pltpu.VMEM((lists_dev, cols), BF16),
            pltpu.VMEM((outers, 1, rows_dev), jnp.int32),
            pltpu.VMEM((members, outers, 1, rows_dev), jnp.int32),
            pltpu.VMEM((outers, rows_dev, cols), BF16),
            pltpu.VMEM((slots, cols), BF16),
            pltpu.VMEM((slots, cols), BF16),
            dma,
            *[dma((outers,))] * 4,
            *[dma((members,))] * 4,
        ],
        compiler_params=pltpu.CompilerParams(
            collective_id=0, has_side_effects=True, vmem_limit_bytes=48 * 2**20
        ),
    )(list_ids.reshape(1, rows_dev), vectors, coarse_centroids)


def halving_plan(members, height, width):
    plan = []
    for _ in range(members.bit_length() - 1):
        if height > 16:
            height //= 2
        else:
            width //= 2
        plan.append((height, width))
    return plan


def quantize_kernel(
    scale,
    sub,
    plan,
    res_ref,
    cent_ref,
    code_ref,
    out_ref,
    grad_ref,
    res_t,
    reb_t,
    back,
    acc,
    *rest,
):
    steps = len(plan)
    arriving, leaving = rest[:steps], rest[steps : 2 * steps]
    sum_send, sum_recv, gather_send, gather_recv, back_send, back_recv = rest[2 * steps :]
    groups, height, width = acc.shape
    per_group = height // sub
    rows_dev = out_ref.shape[0]
    outers = lax.axis_size("outer")
    me, outer = lax.axis_index("member"), lax.axis_index("outer")
    cols = res_ref.shape[1]

    bits = [lax.rem(lax.div(me, 2**step), 2) for step in range(steps)]
    partners = [me + (1 - 2 * bits[step]) * 2**step for step in range(steps)]
    barrier = greet(
        [{"outer": later_on("outer", step)} for step in range(1, outers)]
        + [{"member": partner} for partner in partners]
    )

    starts = [(0, 0)]
    for step, (high, wide) in enumerate(plan):
        row, col = starts[-1]
        was_high = height if step == 0 else plan[step - 1][0]
        if was_high != high:
            starts.append((row + bits[step] * high, col))
        else:
            starts.append((row, col + bits[step] * wide))

    def block(step, start):
        high, wide = plan[step]
        return (
            pl.ds(pl.multiple_of(start[0], 16), high),
            pl.ds(pl.multiple_of(start[1], 128), wide),
        )

    def kept(step):
        return block(step, starts[step + 1])

    def given(step):
        row, col = starts[step]
        kept_row, kept_col = starts[step + 1]
        high, wide = plan[step]
        was_high = height if step == 0 else plan[step - 1][0]
        if was_high != high:
            return block(step, (row + (1 - bits[step]) * high, col))
        return block(step, (row, col + (1 - bits[step]) * wide))

    def sum_copy(step, group):
        return pltpu.make_async_remote_copy(
            src_ref=leaving[step].at[group],
            dst_ref=arriving[step].at[group],
            send_sem=sum_send.at[step, group],
            recv_sem=sum_recv.at[step, group],
            device_id={"member": partners[step]},
            device_id_type=MESH,
        )

    def gather_copy(step, group):
        where = kept(step)
        return pltpu.make_async_remote_copy(
            src_ref=grad_ref.at[group, where[0], where[1]],
            dst_ref=grad_ref.at[group, where[0], where[1]],
            send_sem=gather_send.at[step, group],
            recv_sem=gather_recv.at[step, group],
            device_id={"member": partners[step]},
            device_id_type=MESH,
        )

    def send_sum(step, group):
        rows, columns = given(step)
        leaving[step][group] = acc[group, rows, columns].astype(BF16)
        sum_copy(step, group).start()

    def take_sum(step, group):
        sum_copy(step, group).wait()
        rows, columns = kept(step)
        total = acc[group, rows, columns] + arriving[step][group].astype(F32)
        if step + 1 < steps:
            acc[group, rows, columns] = total
            send_sum(step + 1, group)
        else:
            grad_ref[group, rows, columns] = total.astype(BF16)
            gather_copy(step, group).start()

    def take_gather(step, group):
        gather_copy(step, group).wait()
        if step > 0:
            gather_copy(step - 1, group).start()

    def advance(tick):
        for stage in range(2 * steps, 0, -1):
            group = tick - stage

            @pl.when((group >= 0) & (group < groups))
            def _(stage=stage, group=group):
                if stage <= steps:
                    take_sum(stage - 1, group)
                else:
                    take_gather(2 * steps - stage, group)

    res_t[...] = res_ref[...].astype(F32).T.astype(BF16)
    pl.semaphore_wait(barrier, outers - 1 + steps)

    @pl.loop(0, groups)
    def _(tick):
        for inner in range(per_group):
            space = tick * per_group + inner
            at = pl.ds(pl.multiple_of(space * sub, sub), sub)
            rebuilt_t, grad = one_subspace(code_ref[space], res_t[at, :], scale)
            reb_t[at, :] = rebuilt_t
            acc[tick, inner * sub : (inner + 1) * sub, :] = grad
        advance(tick)
        send_sum(0, tick)

    rebuilt = reb_t[...].T.astype(BF16).astype(F32)
    full = (cent_ref[...].astype(F32) + rebuilt).astype(BF16)
    for source in range(outers):
        back[source] = full[source * rows_dev : (source + 1) * rows_dev, :]
    here = pl.ds(pl.multiple_of(outer * cols, cols), cols)

    def back_copy(step):
        target = later_on("outer", step)
        return pltpu.make_async_remote_copy(
            src_ref=back.at[target],
            dst_ref=out_ref.at[:, here],
            send_sem=back_send.at[step],
            recv_sem=back_recv.at[step],
            device_id={"outer": target},
            device_id_type=MESH,
        )

    for step in range(1, outers):
        back_copy(step).start()
    out_ref[:, here] = back[outer]

    @pl.loop(groups, groups + 2 * steps)
    def _(tick):
        advance(tick)

    for step in range(1, outers):
        back_copy(step).wait()


def quantize(scale, residual, cent, codebook):
    rows, cols = residual.shape
    spaces, sub, codes = codebook.shape
    members, outers = lax.axis_size("member"), lax.axis_size("outer")
    per_group = 1
    while per_group * sub * codes // members < 16 * 128:
        per_group *= 2
    groups, height = spaces // per_group, per_group * sub
    plan = halving_plan(members, height, codes)
    vmem = pl.BlockSpec(memory_space=pltpu.VMEM)
    dma = pltpu.SemaphoreType.DMA
    pieces_moving = [pltpu.VMEM((groups, high, wide), BF16) for high, wide in plan]
    full, grad = pl.pallas_call(
        functools.partial(quantize_kernel, scale, sub, plan),
        out_shape=(
            jax.ShapeDtypeStruct((rows // outers, cols * outers), BF16),
            jax.ShapeDtypeStruct((groups, height, codes), BF16),
        ),
        in_specs=[vmem] * 3,
        out_specs=(vmem, vmem),
        scratch_shapes=[
            pltpu.VMEM((cols, rows), BF16),
            pltpu.VMEM((cols, rows), F32),
            pltpu.VMEM((outers, rows // outers, cols), BF16),
            pltpu.VMEM((groups, height, codes), F32),
            *pieces_moving,
            *pieces_moving,
            *[dma((len(plan), groups))] * 4,
            *[dma((outers,))] * 2,
        ],
        compiler_params=pltpu.CompilerParams(
            collective_id=1, has_side_effects=True, vmem_limit_bytes=48 * 2**20
        ),
    )(residual, cent, codebook)
    return full, grad.reshape(codebook.shape).astype(F32)


def on_device(vectors, list_ids, coarse_centroids, codebook):
    members, outers = lax.axis_size("member"), lax.axis_size("outer")
    residual, cent = fetch(vectors, list_ids, coarse_centroids)
    scale = 2.0 * codebook.shape[2] / (vectors.shape[0] * members * outers)
    return quantize(scale, residual, cent, codebook)


def solution(mesh):
    return jax.shard_map(
        on_device,
        mesh=mesh,
        in_specs=(
            P(("outer", "member"), None),
            P(("outer", "member")),
            P("member", None),
            P("outer", None, None),
        ),
        out_specs=(P(("outer", "member"), None), P("outer", None, None)),
        check_vma=False,
    )
```

```python
import functools
import math

import jax
import jax.numpy as jnp
from jax import lax
from jax.experimental import pallas as pl
from jax.experimental.pallas import tpu as pltpu
from jax.sharding import PartitionSpec as P

MESH = pl.DeviceIdType.MESH
LOG2E = math.log2(math.e)
F32, BF16 = jnp.float32, jnp.bfloat16


def pieces(x):
    hi = x.astype(BF16)
    rest = x - hi.astype(F32)
    mid = rest.astype(BF16)
    low = (rest - mid.astype(F32)).astype(BF16)
    return hi, mid, low


def one_subspace(code, res_t, scale):
    rows = res_t.shape[1]
    codes = code.shape[1]
    code_wide = code.astype(F32)
    norm = (-0.5 * LOG2E) * jnp.sum(code_wide * code_wide, axis=0, keepdims=True)
    hi, mid, low = pieces(norm)
    row_index = lax.broadcasted_iota(jnp.int32, (16, codes), 0)
    tail = jnp.where(
        row_index == 0,
        hi.astype(F32),
        jnp.where(row_index == 1, mid.astype(F32), jnp.where(row_index == 2, low.astype(F32), 0.0)),
    ).astype(BF16)
    right = jnp.concatenate([code, code, code, tail], axis=0)
    ones = jnp.ones((16, rows), BF16)
    left = jnp.concatenate([*pieces(res_t.astype(F32) * LOG2E), ones], axis=0)
    logits = lax.dot_general(left, right, (((0,), (0,)), ((), ())), preferred_element_type=F32)
    top = jnp.max(logits, axis=1, keepdims=True)
    raised = jnp.exp2(logits - top)
    total = jnp.sum(raised, axis=1, keepdims=True)
    weights = (raised * (1.0 / total)).astype(BF16)
    rebuilt_t = lax.dot_general(code, weights, (((1,), (1,)), ((), ())), preferred_element_type=F32)
    sums = jnp.dot(jnp.concatenate([res_t, ones], axis=0), weights, preferred_element_type=F32)
    sub = code.shape[0]
    counts = sums[sub : sub + 1, :]
    return rebuilt_t, scale * (counts * code_wide - sums[:sub, :])


def later_on(axis, step):
    size = lax.axis_size(axis)
    return lax.rem(lax.axis_index(axis) + step, size)


def greet(axis_targets):
    barrier = pltpu.get_barrier_semaphore()
    for target in axis_targets:
        pl.semaphore_signal(barrier, inc=1, device_id=target, device_id_type=MESH)
    return barrier


def split_plan(members, height, width):
    plan, stride = [], 1
    while stride < members:
        left = members // stride
        factor = 2 if stride < 4 or left == 2 else 4
        by_rows = height // factor >= 16
        if by_rows:
            height //= factor
        else:
            width //= factor
        plan.append((factor, stride, by_rows, height, width))
        stride *= factor
    return plan


def step_kernel(
    scale,
    sub,
    capacity,
    plan,
    ids_hbm,
    vec_hbm,
    table_hbm,
    code_hbm,
    out_ref,
    grad_ref,
    ids_own,
    vec_own,
    table,
    code_ref,
    ids_pair,
    ids_all,
    vec_got,
    sent,
    got,
    cent_ref,
    res_t,
    reb_t,
    back,
    acc,
    *rest,
):
    stages = len(plan)
    arriving, leaving = rest[:stages], rest[stages : 2 * stages]
    sum_send, sum_recv = rest[2 * stages : 3 * stages], rest[3 * stages : 4 * stages]
    gather_send, gather_recv = rest[4 * stages : 5 * stages], rest[5 * stages : 6 * stages]
    (
        load_sem,
        table_sem,
        pair_send,
        pair_recv,
        vec_send,
        vec_recv,
        back_send,
        back_recv,
        ids_send,
        ids_recv,
        row_send,
        row_recv,
    ) = rest[6 * stages :]
    members, outers = lax.axis_size("member"), lax.axis_size("outer")
    me, outer = lax.axis_index("member"), lax.axis_index("outer")
    parts, lists_dev, part_cols = table.shape
    cols = parts * part_cols
    rows_dev = vec_own.shape[0]
    block = outers * capacity
    slots = members * block
    groups, height, width = acc.shape
    per_group = height // sub

    def columns_of(index, size):
        return pl.ds(pl.multiple_of(index * size, size), size)

    def block_of(index):
        return pl.ds(pl.multiple_of(index * block, block), block)

    loads = [
        pltpu.make_async_copy(ids_hbm, ids_own, load_sem.at[0]),
        pltpu.make_async_copy(vec_hbm, vec_own, load_sem.at[1]),
        pltpu.make_async_copy(code_hbm, code_ref, load_sem.at[2]),
    ]
    table_copies = [
        pltpu.make_async_copy(
            table_hbm.at[:, columns_of(outer * parts + part, part_cols)],
            table.at[part],
            table_sem.at[part],
        )
        for part in range(parts)
    ]
    loads[0].start()
    loads[1].start()
    for copy in table_copies:
        copy.start()
    loads[2].start()
    barrier = greet([{"outer": later_on("outer", step)} for step in range(1, outers)])

    @pl.loop(1, members)
    def _(step):
        pl.semaphore_signal(
            barrier, inc=1, device_id={"member": later_on("member", step)}, device_id_type=MESH
        )

    loads[0].wait()
    ids_pair[outer] = ids_own[...]
    loads[1].wait()
    here = columns_of(outer, cols)
    vec_got[outer] = vec_own[:, here]
    pl.semaphore_wait(barrier, outers + members - 2)

    def outer_copies(step):
        target = later_on("outer", step)
        ids_copy = pltpu.make_async_remote_copy(
            src_ref=ids_own,
            dst_ref=ids_pair.at[outer],
            send_sem=pair_send.at[step],
            recv_sem=pair_recv.at[step],
            device_id={"outer": target},
            device_id_type=MESH,
        )
        vec_copy = pltpu.make_async_remote_copy(
            src_ref=vec_own.at[:, columns_of(target, cols)],
            dst_ref=vec_got.at[outer],
            send_sem=vec_send.at[step],
            recv_sem=vec_recv.at[step],
            device_id={"outer": target},
            device_id_type=MESH,
        )
        return ids_copy, vec_copy

    outer_pairs = [outer_copies(step) for step in range(1, outers)]
    for ids_copy, _ in outer_pairs:
        ids_copy.start()
    for ids_copy, _ in outer_pairs:
        ids_copy.wait()

    def ids_copy_of(step):
        return pltpu.make_async_remote_copy(
            src_ref=ids_pair,
            dst_ref=ids_all.at[me],
            send_sem=ids_send.at[step],
            recv_sem=ids_recv.at[step],
            device_id={"member": later_on("member", step)},
            device_id_type=MESH,
        )

    @pl.loop(1, members)
    def _(step):
        ids_copy_of(step).start()

    for _, vec_copy in outer_pairs:
        vec_copy.start()

    ids_all[me] = ids_pair[...]
    row_index = lax.broadcasted_iota(jnp.int32, (rows_dev, rows_dev), 0)
    col_index = lax.broadcasted_iota(jnp.int32, (rows_dev, rows_dev), 1)
    before = jnp.where(row_index < col_index, 1.0, 0.0).astype(BF16)
    slot = lax.broadcasted_iota(jnp.int32, (slots, rows_dev), 0)
    slot_rank = lax.rem(slot, capacity).astype(F32)

    def picked(local):
        own = (local >= 0) & (local < lists_dev)
        rank = jnp.dot(jnp.where(own, 1.0, 0.0).astype(BF16), before, preferred_element_type=F32)
        return own & (rank == slot_rank)

    slot_owner = lax.div(slot, block)
    slot_outer = lax.rem(lax.div(slot, capacity), outers)
    places = []
    for source in range(outers):
        wanted = jnp.broadcast_to(ids_pair[source], (slots, rows_dev)) - slot_owner * lists_dev
        place = picked(wanted) & (slot_outer == source)
        places.append(jnp.where(place, 1.0, 0.0).T.astype(BF16))
    place_all = jnp.concatenate(places, axis=0)

    @pl.loop(1, members)
    def _(step):
        ids_copy_of(step).wait()

    ids = ids_all[...].reshape(members * outers, 1, rows_dev)
    ids = jnp.broadcast_to(ids, (members * outers, capacity, rows_dev)).reshape(slots, rows_dev)
    local = ids - me * lists_dev
    index = jnp.sum(jnp.where(picked(local), local.astype(F32), 0.0), axis=1, keepdims=True)
    lists = lax.broadcasted_iota(jnp.int32, (slots, lists_dev), 1)
    onehot = jnp.where(lists == index.astype(jnp.int32), 1.0, 0.0).astype(BF16)

    def row_copy_of(part, step):
        target = later_on("member", step)
        return pltpu.make_async_remote_copy(
            src_ref=sent.at[part, block_of(target)],
            dst_ref=got.at[part, block_of(me)],
            send_sem=row_send.at[part, step],
            recv_sem=row_recv.at[part, step],
            device_id={"member": target},
            device_id_type=MESH,
        )

    for part in range(parts):
        table_copies[part].wait()
        sent[part] = jnp.dot(onehot, table[part], preferred_element_type=F32).astype(BF16)

        @pl.loop(1, members)
        def _(step, part=part):
            row_copy_of(part, step).start()

        got[part, block_of(me)] = sent[part, block_of(me)]

    digits = [lax.rem(lax.div(me, stride), factor) for factor, stride, *_ in plan]

    def partner(stage, step):
        factor, stride = plan[stage][:2]
        digit = digits[stage]
        return me + (lax.rem(digit + step, factor) - digit) * stride

    starts = [(0, 0)]
    for (factor, stride, by_rows, high, wide), digit in zip(plan, digits):
        row, col = starts[-1]
        starts.append((row + digit * high, col) if by_rows else (row, col + digit * wide))

    def place_of(stage, start):
        high, wide = plan[stage][3:]
        return (
            pl.ds(pl.multiple_of(start[0], 16), high),
            pl.ds(pl.multiple_of(start[1], 128), wide),
        )

    def kept(stage):
        return place_of(stage, starts[stage + 1])

    def given(stage, step):
        factor, _, by_rows, high, wide = plan[stage]
        row, col = starts[stage]
        digit = lax.rem(digits[stage] + step, factor)
        return place_of(stage, (row + digit * high, col) if by_rows else (row, col + digit * wide))

    def sum_copy(stage, group, step):
        return pltpu.make_async_remote_copy(
            src_ref=leaving[stage].at[group, step - 1],
            dst_ref=arriving[stage].at[group, step - 1],
            send_sem=sum_send[stage].at[group, step - 1],
            recv_sem=sum_recv[stage].at[group, step - 1],
            device_id={"member": partner(stage, step)},
            device_id_type=MESH,
        )

    def gather_copy(stage, group, step):
        rows, columns = kept(stage)
        return pltpu.make_async_remote_copy(
            src_ref=grad_ref.at[group, rows, columns],
            dst_ref=grad_ref.at[group, rows, columns],
            send_sem=gather_send[stage].at[group, step - 1],
            recv_sem=gather_recv[stage].at[group, step - 1],
            device_id={"member": partner(stage, step)},
            device_id_type=MESH,
        )

    def others(stage):
        return range(1, plan[stage][0])

    def send_sum(stage, group):
        for step in others(stage):
            rows, columns = given(stage, step)
            leaving[stage][group, step - 1] = acc[group, rows, columns].astype(BF16)
            sum_copy(stage, group, step).start()

    def send_gather(stage, group):
        for step in others(stage):
            gather_copy(stage, group, step).start()

    def take_sum(stage, group):
        for step in others(stage):
            sum_copy(stage, group, step).wait()
        rows, columns = kept(stage)
        total = acc[group, rows, columns]
        for step in others(stage):
            total = total + arriving[stage][group, step - 1].astype(F32)
        if stage + 1 < stages:
            acc[group, rows, columns] = total
            send_sum(stage + 1, group)
        else:
            grad_ref[group, rows, columns] = total.astype(BF16)
            send_gather(stage, group)

    def take_gather(stage, group):
        for step in others(stage):
            gather_copy(stage, group, step).wait()
        if stage > 0:
            send_gather(stage - 1, group)

    work = [(take_sum, stage) for stage in range(stages)]
    work += [(take_gather, stage) for stage in reversed(range(stages))]
    lags, lag = [], 0
    for _, stage in work:
        lag += 1 if stage == 0 else 2
        lags.append(lag)

    def advance(tick):
        for (take, stage), lag in reversed(list(zip(work, lags))):
            group = tick - lag

            @pl.when((group >= 0) & (group < groups))
            def _(take=take, stage=stage, group=group):
                take(stage, group)

    for _, vec_copy in outer_pairs:
        vec_copy.wait()
    loads[2].wait()
    part_groups = groups // parts

    @pl.loop(0, parts)
    def _(part):
        @pl.loop(1, members)
        def _(step):
            row_copy_of(part, step).wait()

        cent = jnp.dot(place_all, got[part], preferred_element_type=F32)
        cent_ref[part] = cent.astype(BF16)
        at = columns_of(part, part_cols)
        vec = jnp.concatenate([vec_got[source, :, at] for source in range(outers)], axis=0)
        residual = (vec.astype(F32) - cent).astype(BF16).astype(F32)
        res_t[at, :] = residual.T.astype(BF16)

        @pl.loop(0, part_groups)
        def _(inner_group):
            tick = part * part_groups + inner_group
            for inner in range(per_group):
                space = tick * per_group + inner
                at = pl.ds(pl.multiple_of(space * sub, sub), sub)
                rebuilt_t, grad = one_subspace(code_ref[space], res_t[at, :], scale)
                reb_t[at, :] = rebuilt_t
                acc[tick, inner * sub : (inner + 1) * sub, :] = grad
            advance(tick)
            send_sum(0, tick)

    rebuilt = reb_t[...].T.astype(BF16).astype(F32)
    for part in range(parts):
        at = slice(part * part_cols, (part + 1) * part_cols)
        full = (cent_ref[part].astype(F32) + rebuilt[:, at]).astype(BF16)
        for source in range(outers):
            back[source, :, at] = full[source * rows_dev : (source + 1) * rows_dev, :]

    def back_copy(step):
        target = later_on("outer", step)
        return pltpu.make_async_remote_copy(
            src_ref=back.at[target],
            dst_ref=out_ref.at[:, here],
            send_sem=back_send.at[step],
            recv_sem=back_recv.at[step],
            device_id={"outer": target},
            device_id_type=MESH,
        )

    for step in range(1, outers):
        back_copy(step).start()
    out_ref[:, here] = back[outer]

    @pl.loop(groups, groups + lags[-1])
    def _(tick):
        advance(tick)

    for step in range(1, outers):
        back_copy(step).wait()


PARTS = 2


def on_device(vectors, list_ids, coarse_centroids, codebook):
    rows_dev, row_width = vectors.shape
    members, outers = lax.axis_size("member"), lax.axis_size("outer")
    lists_dev = coarse_centroids.shape[0]
    capacity = max(2 * rows_dev // members, 16 // outers, 8)
    cols = row_width // outers
    slots = members * outers * capacity
    rows = outers * rows_dev
    spaces, sub, codes = codebook.shape
    scale = 2.0 * codes / (rows_dev * members * outers)
    per_group = 1
    while per_group * sub * codes // members < 16 * 128:
        per_group *= 2
    groups, height = spaces // per_group, per_group * sub
    parts = min(PARTS, groups, cols // 128)
    part_cols = cols // parts
    plan = split_plan(members, height, codes)
    vmem = pl.BlockSpec(memory_space=pltpu.VMEM)
    anywhere = pl.BlockSpec(memory_space=pl.ANY)
    dma = pltpu.SemaphoreType.DMA
    moving = [pltpu.VMEM((groups, item[0] - 1, item[3], item[4]), BF16) for item in plan]
    moving_sems = [dma((groups, item[0] - 1)) for item in plan]
    full, grad = pl.pallas_call(
        functools.partial(step_kernel, scale, sub, capacity, plan),
        out_shape=(
            jax.ShapeDtypeStruct((rows_dev, row_width), BF16),
            jax.ShapeDtypeStruct((groups, height, codes), BF16),
        ),
        in_specs=[anywhere] * 4,
        out_specs=(vmem, vmem),
        scratch_shapes=[
            pltpu.VMEM((1, rows_dev), jnp.int32),
            pltpu.VMEM((rows_dev, row_width), BF16),
            pltpu.VMEM((parts, lists_dev, part_cols), BF16),
            pltpu.VMEM(codebook.shape, BF16),
            pltpu.VMEM((outers, 1, rows_dev), jnp.int32),
            pltpu.VMEM((members, outers, 1, rows_dev), jnp.int32),
            pltpu.VMEM((outers, rows_dev, cols), BF16),
            pltpu.VMEM((parts, slots, part_cols), BF16),
            pltpu.VMEM((parts, slots, part_cols), BF16),
            pltpu.VMEM((parts, rows, part_cols), BF16),
            pltpu.VMEM((cols, rows), BF16),
            pltpu.VMEM((cols, rows), F32),
            pltpu.VMEM((outers, rows_dev, cols), BF16),
            pltpu.VMEM((groups, height, codes), F32),
            *moving,
            *moving,
            *moving_sems * 4,
            dma((3,)),
            dma((parts,)),
            *[dma((outers,))] * 6,
            *[dma((members,))] * 2,
            *[dma((parts, members))] * 2,
        ],
        compiler_params=pltpu.CompilerParams(
            collective_id=0, has_side_effects=True, vmem_limit_bytes=52 * 2**20
        ),
    )(list_ids.reshape(1, rows_dev), vectors, coarse_centroids, codebook)
    return full, grad.reshape(codebook.shape).astype(F32)


def solution(mesh):
    return jax.shard_map(
        on_device,
        mesh=mesh,
        in_specs=(
            P(("outer", "member"), None),
            P(("outer", "member")),
            P("member", None),
            P("outer", None, None),
        ),
        out_specs=(P(("outer", "member"), None), P("outer", None, None)),
        check_vma=False,
    )
```

```python
import functools
import math

import jax
import jax.numpy as jnp
from jax import lax
from jax.experimental import pallas as pl
from jax.experimental.pallas import tpu as pltpu
from jax.sharding import PartitionSpec as P

MESH = pl.DeviceIdType.MESH
LOG2E = math.log2(math.e)
F32, BF16 = jnp.float32, jnp.bfloat16


def pieces(x):
    hi = x.astype(BF16)
    rest = x - hi.astype(F32)
    mid = rest.astype(BF16)
    low = (rest - mid.astype(F32)).astype(BF16)
    return hi, mid, low


def code_operand(code):
    code_wide = code.astype(F32)
    norm = (-0.5 * LOG2E) * jnp.sum(code_wide * code_wide, axis=0, keepdims=True)
    hi, mid, low = pieces(norm)
    row_index = lax.broadcasted_iota(jnp.int32, (16, code.shape[1]), 0)
    tail = jnp.where(
        row_index == 0,
        hi.astype(F32),
        jnp.where(row_index == 1, mid.astype(F32), jnp.where(row_index == 2, low.astype(F32), 0.0)),
    ).astype(BF16)
    return jnp.concatenate([code, code, code, tail], axis=0)


def one_subspace(code, right, res_t, scale):
    rows = res_t.shape[1]
    code_wide = code.astype(F32)
    ones = jnp.ones((16, rows), BF16)
    left = jnp.concatenate([*pieces(res_t.astype(F32) * LOG2E), ones], axis=0)
    logits = lax.dot_general(left, right, (((0,), (0,)), ((), ())), preferred_element_type=F32)
    top = jnp.max(logits, axis=1, keepdims=True)
    raised = jnp.exp2(logits - top)
    total = jnp.sum(raised, axis=1, keepdims=True)
    weights = (raised * (1.0 / total)).astype(BF16)
    rebuilt_t = lax.dot_general(code, weights, (((1,), (1,)), ((), ())), preferred_element_type=F32)
    sums = jnp.dot(jnp.concatenate([res_t, ones], axis=0), weights, preferred_element_type=F32)
    sub = code.shape[0]
    counts = sums[sub : sub + 1, :]
    return rebuilt_t, scale * (counts * code_wide - sums[:sub, :])


def later_on(axis, step):
    size = lax.axis_size(axis)
    return lax.rem(lax.axis_index(axis) + step, size)


def greet(axis_targets):
    barrier = pltpu.get_barrier_semaphore()
    for target in axis_targets:
        pl.semaphore_signal(barrier, inc=1, device_id=target, device_id_type=MESH)
    return barrier


def split_plan(members, height, width):
    plan, stride = [], 1
    while stride < members:
        left = members // stride
        factor = 2 if stride < 4 or left == 2 else 4
        by_rows = height // factor >= 16
        if by_rows:
            height //= factor
        else:
            width //= factor
        plan.append((factor, stride, by_rows, height, width))
        stride *= factor
    return plan


def step_kernel(
    scale,
    sub,
    capacity,
    plan,
    ids_hbm,
    vec_hbm,
    table_hbm,
    code_hbm,
    out_ref,
    grad_ref,
    ids_own,
    vec_own,
    table,
    code_ref,
    ids_pair,
    ids_all,
    vec_got,
    sent,
    got,
    cent_ref,
    res_t,
    reb_t,
    back,
    acc,
    right_ref,
    *rest,
):
    stages = len(plan)
    arriving, leaving = rest[:stages], rest[stages : 2 * stages]
    sum_send, sum_recv = rest[2 * stages : 3 * stages], rest[3 * stages : 4 * stages]
    gather_send, gather_recv = rest[4 * stages : 5 * stages], rest[5 * stages : 6 * stages]
    (
        load_sem,
        table_sem,
        pair_send,
        pair_recv,
        vec_send,
        vec_recv,
        back_send,
        back_recv,
        ids_send,
        ids_recv,
        row_send,
        row_recv,
    ) = rest[6 * stages :]
    members, outers = lax.axis_size("member"), lax.axis_size("outer")
    me, outer = lax.axis_index("member"), lax.axis_index("outer")
    parts, lists_dev, part_cols = table.shape
    cols = parts * part_cols
    rows_dev = vec_own.shape[0]
    block = outers * capacity
    slots = members * block
    groups, height, width = acc.shape
    per_group = height // sub

    def columns_of(index, size):
        return pl.ds(pl.multiple_of(index * size, size), size)

    def block_of(index):
        return pl.ds(pl.multiple_of(index * block, block), block)

    loads = [
        pltpu.make_async_copy(ids_hbm, ids_own, load_sem.at[0]),
        pltpu.make_async_copy(vec_hbm, vec_own, load_sem.at[1]),
        pltpu.make_async_copy(code_hbm, code_ref, load_sem.at[2]),
    ]
    table_copies = [
        pltpu.make_async_copy(
            table_hbm.at[:, columns_of(outer * parts + part, part_cols)],
            table.at[part],
            table_sem.at[part],
        )
        for part in range(parts)
    ]
    loads[0].start()
    loads[1].start()
    for copy in table_copies:
        copy.start()
    loads[2].start()
    barrier = greet([{"outer": later_on("outer", step)} for step in range(1, outers)])

    @pl.loop(1, members)
    def _(step):
        pl.semaphore_signal(
            barrier, inc=1, device_id={"member": later_on("member", step)}, device_id_type=MESH
        )

    loads[0].wait()
    ids_pair[outer] = ids_own[...]
    loads[1].wait()
    here = columns_of(outer, cols)
    vec_got[outer] = vec_own[:, here]
    pl.semaphore_wait(barrier, outers + members - 2)

    def outer_copies(step):
        target = later_on("outer", step)
        ids_copy = pltpu.make_async_remote_copy(
            src_ref=ids_own,
            dst_ref=ids_pair.at[outer],
            send_sem=pair_send.at[step],
            recv_sem=pair_recv.at[step],
            device_id={"outer": target},
            device_id_type=MESH,
        )
        vec_copy = pltpu.make_async_remote_copy(
            src_ref=vec_own.at[:, columns_of(target, cols)],
            dst_ref=vec_got.at[outer],
            send_sem=vec_send.at[step],
            recv_sem=vec_recv.at[step],
            device_id={"outer": target},
            device_id_type=MESH,
        )
        return ids_copy, vec_copy

    outer_pairs = [outer_copies(step) for step in range(1, outers)]
    for ids_copy, _ in outer_pairs:
        ids_copy.start()
    for ids_copy, _ in outer_pairs:
        ids_copy.wait()

    def ids_copy_of(step):
        return pltpu.make_async_remote_copy(
            src_ref=ids_pair,
            dst_ref=ids_all.at[me],
            send_sem=ids_send.at[step],
            recv_sem=ids_recv.at[step],
            device_id={"member": later_on("member", step)},
            device_id_type=MESH,
        )

    @pl.loop(1, members)
    def _(step):
        ids_copy_of(step).start()

    for _, vec_copy in outer_pairs:
        vec_copy.start()

    ids_all[me] = ids_pair[...]
    row_index = lax.broadcasted_iota(jnp.int32, (rows_dev, rows_dev), 0)
    col_index = lax.broadcasted_iota(jnp.int32, (rows_dev, rows_dev), 1)
    before = jnp.where(row_index < col_index, 1.0, 0.0).astype(BF16)
    slot = lax.broadcasted_iota(jnp.int32, (slots, rows_dev), 0)
    slot_rank = lax.rem(slot, capacity).astype(F32)

    def picked(local):
        own = (local >= 0) & (local < lists_dev)
        rank = jnp.dot(jnp.where(own, 1.0, 0.0).astype(BF16), before, preferred_element_type=F32)
        return own & (rank == slot_rank)

    slot_owner = lax.div(slot, block)
    slot_outer = lax.rem(lax.div(slot, capacity), outers)
    places = []
    for source in range(outers):
        wanted = jnp.broadcast_to(ids_pair[source], (slots, rows_dev)) - slot_owner * lists_dev
        place = picked(wanted) & (slot_outer == source)
        places.append(jnp.where(place, 1.0, 0.0).T.astype(BF16))
    place_all = jnp.concatenate(places, axis=0)
    loads[2].wait()
    spaces = code_ref.shape[0]

    @pl.loop(0, spaces // 2)
    def _(space):
        right_ref[space] = code_operand(code_ref[space])

    @pl.loop(1, members)
    def _(step):
        ids_copy_of(step).wait()

    ids = ids_all[...].reshape(members * outers, 1, rows_dev)
    ids = jnp.broadcast_to(ids, (members * outers, capacity, rows_dev)).reshape(slots, rows_dev)
    local = ids - me * lists_dev
    index = jnp.sum(jnp.where(picked(local), local.astype(F32), 0.0), axis=1, keepdims=True)
    lists = lax.broadcasted_iota(jnp.int32, (slots, lists_dev), 1)
    onehot = jnp.where(lists == index.astype(jnp.int32), 1.0, 0.0).astype(BF16)

    def row_copy_of(part, step):
        target = later_on("member", step)
        return pltpu.make_async_remote_copy(
            src_ref=sent.at[part, block_of(target)],
            dst_ref=got.at[part, block_of(me)],
            send_sem=row_send.at[part, step],
            recv_sem=row_recv.at[part, step],
            device_id={"member": target},
            device_id_type=MESH,
        )

    for part in range(parts):
        table_copies[part].wait()
        sent[part] = jnp.dot(onehot, table[part], preferred_element_type=F32).astype(BF16)

        @pl.loop(1, members)
        def _(step, part=part):
            row_copy_of(part, step).start()

        got[part, block_of(me)] = sent[part, block_of(me)]

    digits = [lax.rem(lax.div(me, stride), factor) for factor, stride, *_ in plan]

    def partner(stage, step):
        factor, stride = plan[stage][:2]
        digit = digits[stage]
        return me + (lax.rem(digit + step, factor) - digit) * stride

    starts = [(0, 0)]
    for (factor, stride, by_rows, high, wide), digit in zip(plan, digits):
        row, col = starts[-1]
        starts.append((row + digit * high, col) if by_rows else (row, col + digit * wide))

    def place_of(stage, start):
        high, wide = plan[stage][3:]
        return (
            pl.ds(pl.multiple_of(start[0], 16), high),
            pl.ds(pl.multiple_of(start[1], 128), wide),
        )

    def kept(stage):
        return place_of(stage, starts[stage + 1])

    def given(stage, step):
        factor, _, by_rows, high, wide = plan[stage]
        row, col = starts[stage]
        digit = lax.rem(digits[stage] + step, factor)
        return place_of(stage, (row + digit * high, col) if by_rows else (row, col + digit * wide))

    def sum_copy(stage, group, step):
        return pltpu.make_async_remote_copy(
            src_ref=leaving[stage].at[group, step - 1],
            dst_ref=arriving[stage].at[group, step - 1],
            send_sem=sum_send[stage].at[group, step - 1],
            recv_sem=sum_recv[stage].at[group, step - 1],
            device_id={"member": partner(stage, step)},
            device_id_type=MESH,
        )

    def gather_copy(stage, group, step):
        rows, columns = kept(stage)
        return pltpu.make_async_remote_copy(
            src_ref=grad_ref.at[group, rows, columns],
            dst_ref=grad_ref.at[group, rows, columns],
            send_sem=gather_send[stage].at[group, step - 1],
            recv_sem=gather_recv[stage].at[group, step - 1],
            device_id={"member": partner(stage, step)},
            device_id_type=MESH,
        )

    def others(stage):
        return range(1, plan[stage][0])

    def send_sum(stage, group):
        for step in others(stage):
            rows, columns = given(stage, step)
            leaving[stage][group, step - 1] = acc[group, rows, columns].astype(BF16)
            sum_copy(stage, group, step).start()

    def send_gather(stage, group):
        for step in others(stage):
            gather_copy(stage, group, step).start()

    def take_sum(stage, group):
        for step in others(stage):
            sum_copy(stage, group, step).wait()
        rows, columns = kept(stage)
        total = acc[group, rows, columns]
        for step in others(stage):
            total = total + arriving[stage][group, step - 1].astype(F32)
        if stage + 1 < stages:
            acc[group, rows, columns] = total
            send_sum(stage + 1, group)
        else:
            grad_ref[group, rows, columns] = total.astype(BF16)
            send_gather(stage, group)

    def take_gather(stage, group):
        for step in others(stage):
            gather_copy(stage, group, step).wait()
        if stage > 0:
            send_gather(stage - 1, group)

    work = [(take_sum, stage) for stage in range(stages)]
    work += [(take_gather, stage) for stage in reversed(range(stages))]
    lags, lag = [], 0
    for _, stage in work:
        lag += 1 if stage == 0 else 2
        lags.append(lag)

    def advance(tick):
        for (take, stage), lag in zip(work, lags):
            group = tick - lag

            @pl.when((group >= 0) & (group < groups))
            def _(take=take, stage=stage, group=group):
                take(stage, group)

    for _, vec_copy in outer_pairs:
        vec_copy.wait()

    @pl.loop(spaces // 2, spaces)
    def _(space):
        right_ref[space] = code_operand(code_ref[space])

    part_groups = groups // parts

    @pl.loop(0, parts)
    def _(part):
        @pl.loop(1, members)
        def _(step):
            row_copy_of(part, step).wait()

        cent = jnp.dot(place_all, got[part], preferred_element_type=F32)
        cent_ref[part] = cent.astype(BF16)
        at = columns_of(part, part_cols)
        vec = jnp.concatenate([vec_got[source, :, at] for source in range(outers)], axis=0)
        residual = (vec.astype(F32) - cent).astype(BF16).astype(F32)
        res_t[at, :] = residual.T.astype(BF16)

        @pl.loop(0, part_groups)
        def _(inner_group):
            tick = part * part_groups + inner_group
            for inner in range(per_group):
                space = tick * per_group + inner
                at = pl.ds(pl.multiple_of(space * sub, sub), sub)
                rebuilt_t, grad = one_subspace(
                    code_ref[space], right_ref[space], res_t[at, :], scale
                )
                reb_t[at, :] = rebuilt_t
                acc[tick, inner * sub : (inner + 1) * sub, :] = grad
            advance(tick)
            send_sum(0, tick)

    rebuilt = reb_t[...].T.astype(BF16).astype(F32)
    for part in range(parts):
        at = slice(part * part_cols, (part + 1) * part_cols)
        full = (cent_ref[part].astype(F32) + rebuilt[:, at]).astype(BF16)
        for source in range(outers):
            back[source, :, at] = full[source * rows_dev : (source + 1) * rows_dev, :]

    def back_copy(step):
        target = later_on("outer", step)
        return pltpu.make_async_remote_copy(
            src_ref=back.at[target],
            dst_ref=out_ref.at[:, here],
            send_sem=back_send.at[step],
            recv_sem=back_recv.at[step],
            device_id={"outer": target},
            device_id_type=MESH,
        )

    for step in range(1, outers):
        back_copy(step).start()
    out_ref[:, here] = back[outer]

    @pl.loop(groups, groups + lags[-1])
    def _(tick):
        advance(tick)

    for step in range(1, outers):
        back_copy(step).wait()


PARTS = 4


def on_device(vectors, list_ids, coarse_centroids, codebook):
    rows_dev, row_width = vectors.shape
    members, outers = lax.axis_size("member"), lax.axis_size("outer")
    lists_dev = coarse_centroids.shape[0]
    capacity = max(2 * rows_dev // members, 16 // outers, 8)
    cols = row_width // outers
    slots = members * outers * capacity
    rows = outers * rows_dev
    spaces, sub, codes = codebook.shape
    scale = 2.0 * codes / (rows_dev * members * outers)
    per_group = 1
    while per_group * sub * codes // members < 16 * 128:
        per_group *= 2
    groups, height = spaces // per_group, per_group * sub
    parts = min(PARTS, groups, cols // 128)
    part_cols = cols // parts
    plan = split_plan(members, height, codes)
    vmem = pl.BlockSpec(memory_space=pltpu.VMEM)
    anywhere = pl.BlockSpec(memory_space=pl.ANY)
    dma = pltpu.SemaphoreType.DMA
    moving = [pltpu.VMEM((groups, item[0] - 1, item[3], item[4]), BF16) for item in plan]
    moving_sems = [dma((groups, item[0] - 1)) for item in plan]
    full, grad = pl.pallas_call(
        functools.partial(step_kernel, scale, sub, capacity, plan),
        out_shape=(
            jax.ShapeDtypeStruct((rows_dev, row_width), BF16),
            jax.ShapeDtypeStruct((groups, height, codes), BF16),
        ),
        in_specs=[anywhere] * 4,
        out_specs=(vmem, vmem),
        scratch_shapes=[
            pltpu.VMEM((1, rows_dev), jnp.int32),
            pltpu.VMEM((rows_dev, row_width), BF16),
            pltpu.VMEM((parts, lists_dev, part_cols), BF16),
            pltpu.VMEM(codebook.shape, BF16),
            pltpu.VMEM((outers, 1, rows_dev), jnp.int32),
            pltpu.VMEM((members, outers, 1, rows_dev), jnp.int32),
            pltpu.VMEM((outers, rows_dev, cols), BF16),
            pltpu.VMEM((parts, slots, part_cols), BF16),
            pltpu.VMEM((parts, slots, part_cols), BF16),
            pltpu.VMEM((parts, rows, part_cols), BF16),
            pltpu.VMEM((cols, rows), BF16),
            pltpu.VMEM((cols, rows), F32),
            pltpu.VMEM((outers, rows_dev, cols), BF16),
            pltpu.VMEM((groups, height, codes), F32),
            pltpu.VMEM((spaces, 3 * sub + 16, codes), BF16),
            *moving,
            *moving,
            *moving_sems * 4,
            dma((3,)),
            dma((parts,)),
            *[dma((outers,))] * 6,
            *[dma((members,))] * 2,
            *[dma((parts, members))] * 2,
        ],
        compiler_params=pltpu.CompilerParams(
            collective_id=0, has_side_effects=True, vmem_limit_bytes=60 * 2**20
        ),
    )(list_ids.reshape(1, rows_dev), vectors, coarse_centroids, codebook)
    return full, grad.reshape(codebook.shape).astype(F32)


def solution(mesh):
    return jax.shard_map(
        on_device,
        mesh=mesh,
        in_specs=(
            P(("outer", "member"), None),
            P(("outer", "member")),
            P("member", None),
            P("outer", None, None),
        ),
        out_specs=(P(("outer", "member"), None), P("outer", None, None)),
        check_vma=False,
    )
```
